32 devices in a mesh: grp: 8 (over z, y), row: 4 (over x, core).
Axes of the slice: x: 2, y: 2, z: 4, core: 2. Of those that a mesh axis runs over, the one named last changes fastest.
Arguments:
- grads: float32 [12, 4, 1792, 1024], P(None, 'row', 'grp'), may hold values from -320 to 320
- momentum: float32 [12, 4, 1792, 1024], P(None, 'row', 'grp'), may hold values from -640 to 640
- owner_table: int32 [12], replicated, may hold values from 0 to 8, as said below
Outputs:
- new_momentum: float32 [12, 4, 1792, 1024], P(None, 'row', 'grp')
- update: float32 [12, 4, 1792, 1024], P(None, 'row', 'grp')
The draws below stay inside these ranges and needn't reach their ends.
Inputs may be any that keep to these rules, and one draw needn't show every extreme that they name: `owner_table`: each value 0 to 7 appears exactly once; the other entries equal 8.
All inputs are finite; a program needn't handle non-finite values.
Results may differ from the reference program's by a relative error of at most 0.0001.
Values sent between devices are 32-bit elements; how exact they have to be, the bound alone decides.
A program may use at most 128 MiB of HBM per device.

```python
import math
import jax
import jax.numpy as jnp
from jax import lax

ROWS = 7168
C = 1024
ITERS = 2
GROUPS = 8
BLOCKS = 4
MATS = 12
BLOCK_ROWS = 1792


def shared_scales(key, spread):
    key_rows, key_cols = jax.random.split(key)
    row_scale = jnp.exp(jax.random.uniform(key_rows, (MATS, ROWS), jnp.float32, 0.0, math.log(spread)))
    col_scale = jnp.exp(jax.random.uniform(key_cols, (MATS, C), jnp.float32, 0.0, math.log(spread)))
    return (row_scale, col_scale)


def assemble(noise, row_scale, col_scale, rise, factor):
    grade = jnp.arange(ROWS, dtype=jnp.float32) / (ROWS - 1)
    lift = rise ** (0.5 * grade)
    rows_total = (row_scale * lift[None, :]).reshape(MATS, BLOCKS, BLOCK_ROWS, 1)
    return jnp.clip(noise, -4.0, 4.0) * rows_total * col_scale[:, None, None, :] * factor


def draw_grads(key, part):
    row_scale, col_scale = shared_scales(key, 10.0)
    key = jax.random.fold_in(key, 11)
    shape = (MATS, BLOCKS, BLOCK_ROWS, C)
    noise = jax.random.normal(key, shape, jnp.float32)
    return assemble(noise, row_scale, col_scale, 3.0, 0.1)


def draw_momentum(key, part):
    row_scale, col_scale = shared_scales(key, 10.0)
    key = jax.random.fold_in(key, 12)
    shape = (MATS, BLOCKS, BLOCK_ROWS, C)
    noise = jax.random.normal(key, shape, jnp.float32)
    return assemble(noise, row_scale, col_scale, 3.0, 0.2)


def draw_owner_table(key, part):
    key = jax.random.fold_in(key, 13)
    order = jax.random.permutation(key, MATS).astype(jnp.int32)
    return jnp.minimum(order, GROUPS).astype(jnp.int32)


def setup_inputs(seed: int = 0) -> dict:
    splits = jax.random.split(jax.random.key(seed), 4)
    grads = draw_grads(jax.random.fold_in(splits[3], 71), 0)
    momentum = draw_momentum(jax.random.fold_in(splits[3], 71), 0)
    owner_table = draw_owner_table(jax.random.fold_in(splits[3], 71), 0)
    return {"grads": grads, "momentum": momentum, "owner_table": owner_table}


momentum_decay = 0.95
norm_epsilon = 1e-07
first_coef = 3.4445
second_coef = -4.775
third_coef = 2.0315

def high_dot(left, right):
    return jnp.dot(left, right, precision=lax.Precision.HIGHEST, preferred_element_type=jnp.float32)

def newton(matrix):
    total = jnp.sum(matrix * matrix)
    current = matrix / (jnp.sqrt(total) + norm_epsilon)
    for step in range(ITERS):
        gram = high_dot(current.T, current)
        product = high_dot(current, gram)
        current = first_coef * current + second_coef * product + third_coef * high_dot(product, gram)
    return current * (0.2 * math.sqrt(max(ROWS, C)))

def reference(grads, momentum, owner_table):
    in_window = owner_table < GROUPS
    flags = in_window[:, None, None, None]
    new_momentum = jnp.where(flags, momentum_decay * momentum + grads, momentum)
    nesterov = grads + momentum_decay * new_momentum
    group_ids = jnp.arange(GROUPS, dtype=jnp.int32)
    matches = (owner_table[None, :] == group_ids[:, None]).astype(jnp.int32)
    chosen = lax.optimization_barrier(jnp.sum(matches * jnp.arange(MATS, dtype=jnp.int32)[None, :], axis=1)).astype(jnp.int32)
    selected = jnp.take(nesterov, chosen, axis=0)

    def one_matrix(stack):
        return newton(stack.reshape(ROWS, C)).reshape(BLOCKS, BLOCK_ROWS, C)
    results = lax.map(one_matrix, selected)
    picked = jnp.take(results, jnp.minimum(owner_table, GROUPS - 1).astype(jnp.int32), axis=0)
    update = jnp.where(flags, picked, jnp.zeros_like(picked))
    return (new_momentum, update)
```

```python
import math

import jax
import jax.numpy as jnp
from jax import lax
from jax.experimental import pallas as pl
from jax.experimental.pallas import tpu as pltpu
from jax.sharding import Mesh
from jax.sharding import PartitionSpec as P

momentum_decay = 0.95
norm_epsilon = 1e-07
first_coef = 3.4445
second_coef = -4.775
third_coef = 2.0315

STRIPES = 4


def dot3(left, right, dims=(((1,), (0,)), ((), ()))):
    return lax.dot_general(
        left, right, dims, precision=lax.Precision.HIGH, preferred_element_type=jnp.float32
    )


def pick_kernel(chosen_ref, grads_ref, momentum_ref, out_ref):
    grad = grads_ref[0, 0]
    out_ref[0] = grad + momentum_decay * (momentum_decay * momentum_ref[0, 0] + grad)


def pick_nesterov(chosen, grads, momentum, groups):
    rows, width = grads.shape[2:]
    state = pl.BlockSpec((1, 1, rows, width), lambda g, chosen: (chosen[g], 0, 0, 0))
    return pl.pallas_call(
        pick_kernel,
        grid_spec=pltpu.PrefetchScalarGridSpec(
            num_scalar_prefetch=1,
            grid=(groups,),
            in_specs=[state, state],
            out_specs=pl.BlockSpec((1, rows, width), lambda g, chosen: (g, 0, 0)),
        ),
        out_shape=jax.ShapeDtypeStruct((groups, rows, width), jnp.float32),
        cost_estimate=pl.CostEstimate(
            flops=4 * groups * rows * width, bytes_accessed=12 * groups * rows * width, transcendentals=0
        ),
    )(chosen, grads, momentum)


def place_kernel(groups, owner_ref, returned_ref, out_ref):
    inside = owner_ref[pl.program_id(0)] < groups

    @pl.when(inside)
    def _():
        out_ref[0, 0] = returned_ref[0]

    @pl.when(jnp.logical_not(inside))
    def _():
        out_ref[...] = jnp.zeros_like(out_ref)


def place_update(owner_table, returned, mats):
    groups, rows, width = returned.shape

    def kernel(*refs):
        place_kernel(groups, *refs)

    return pl.pallas_call(
        kernel,
        grid_spec=pltpu.PrefetchScalarGridSpec(
            num_scalar_prefetch=1,
            grid=(mats,),
            in_specs=[
                pl.BlockSpec(
                    (1, rows, width), lambda k, owner: (jnp.minimum(owner[k], groups - 1), 0, 0)
                )
            ],
            out_specs=pl.BlockSpec((1, 1, rows, width), lambda k, owner: (k, 0, 0, 0)),
        ),
        out_shape=jax.ShapeDtypeStruct((mats, 1, rows, width), jnp.float32),
        cost_estimate=pl.CostEstimate(
            flops=0, bytes_accessed=4 * (groups + mats) * rows * width, transcendentals=0
        ),
    )(owner_table, returned)


def upper_gram(current):
    width = current.shape[1]
    size = width // STRIPES
    return jnp.concatenate(
        [
            dot3(
                current[:, i * size : (i + 1) * size],
                current[:, i * size :],
                (((0,), (0,)), ((), ())),
            )
            for i in range(STRIPES)
        ],
        axis=1,
    )


def whole_gram(packed):
    size = packed.shape[0]
    stripes, at = [], 0
    for i in range(STRIPES):
        stripes.append(packed[:, at : at + (STRIPES - i) * size])
        at += (STRIPES - i) * size
    rows = []
    for i in range(STRIPES):
        below = [stripes[j][:, (i - j) * size : (i - j + 1) * size].T for j in range(i)]
        rows.append(jnp.concatenate(below + [stripes[i]], axis=1))
    return jnp.concatenate(rows, axis=0)


def shards(grads, momentum, owner_table):
    mats = grads.shape[0]
    groups = lax.axis_size("far") * lax.axis_size("near")
    blocks = lax.axis_size("row")
    near = ("near", "row")
    in_window = owner_table < groups
    flags = in_window[:, None, None, None]
    group_ids = jnp.arange(groups, dtype=jnp.int32)
    matches = (owner_table[None, :] == group_ids[:, None]).astype(jnp.int32)
    chosen = jnp.sum(matches * jnp.arange(mats, dtype=jnp.int32)[None, :], axis=1)
    outgoing = pick_nesterov(chosen, grads, momentum, groups)
    rows, width = outgoing.shape[1:]
    owned = lax.all_to_all(outgoing, near, split_axis=0, concat_axis=0, tiled=True)
    new_momentum = jnp.where(flags, momentum_decay * momentum + grads, momentum)
    current = owned.reshape(groups * rows, width)
    scale = 0.2 * math.sqrt(max(rows * groups * blocks, width))
    gram = whole_gram(lax.psum(upper_gram(current), "far"))
    inverse = 1.0 / (jnp.sqrt(jnp.trace(gram)) + norm_epsilon)
    gram = gram * (inverse * inverse)
    low = second_coef * gram + third_coef * dot3(gram, gram)
    gram = first_coef * gram + dot3(gram, low)
    gram = first_coef * gram + dot3(gram, low)
    high = second_coef * gram + third_coef * dot3(gram, gram)
    rest = first_coef * (low + high) + dot3(low, high)
    factor = inverse * scale
    result = (first_coef * first_coef * factor) * current + dot3(current, rest * factor)
    returned = lax.all_to_all(
        result.reshape(groups, rows, width), near, split_axis=0, concat_axis=0, tiled=True
    )
    update = place_update(owner_table, returned, mats)
    return (new_momentum, update)


def solution(mesh):
    groups, blocks = mesh.shape["grp"], mesh.shape["row"]
    near = max(1, groups // blocks)
    assert near * blocks == groups
    split = Mesh(mesh.devices.reshape(groups // near, near, blocks), ("far", "near", "row"))
    spec = P(None, "row", ("far", "near"), None)
    return jax.shard_map(
        shards, mesh=split, in_specs=(spec, spec, P()), out_specs=(spec, spec), check_vma=False
    )
```

```python
import math

import jax
import jax.numpy as jnp
from jax import lax
from jax.experimental import pallas as pl
from jax.experimental.pallas import tpu as pltpu
from jax.sharding import Mesh
from jax.sharding import PartitionSpec as P

momentum_decay = 0.95
norm_epsilon = 1e-07
first_coef = 3.4445
second_coef = -4.775
third_coef = 2.0315

STRIPES = 4


def dot3(left, right, dims=(((1,), (0,)), ((), ()))):
    return lax.dot_general(
        left, right, dims, precision=lax.Precision.HIGH, preferred_element_type=jnp.float32
    )


def pick_kernel(chosen_ref, grads_ref, momentum_ref, out_ref):
    grad = grads_ref[0, 0]
    out_ref[0] = grad + momentum_decay * (momentum_decay * momentum_ref[0, 0] + grad)


def pick_nesterov(chosen, grads, momentum, groups):
    rows, width = grads.shape[2:]
    state = pl.BlockSpec((1, 1, rows, width), lambda g, chosen: (chosen[g], 0, 0, 0))
    return pl.pallas_call(
        pick_kernel,
        grid_spec=pltpu.PrefetchScalarGridSpec(
            num_scalar_prefetch=1,
            grid=(groups,),
            in_specs=[state, state],
            out_specs=pl.BlockSpec((1, rows, width), lambda g, chosen: (g, 0, 0)),
        ),
        out_shape=jax.ShapeDtypeStruct((groups, rows, width), jnp.float32),
        cost_estimate=pl.CostEstimate(
            flops=4 * groups * rows * width, bytes_accessed=12 * groups * rows * width, transcendentals=0
        ),
    )(chosen, grads, momentum)


def place_kernel(groups, owner_ref, returned_ref, out_ref):
    inside = owner_ref[pl.program_id(0)] < groups

    @pl.when(inside)
    def _():
        out_ref[0, 0] = returned_ref[0]

    @pl.when(jnp.logical_not(inside))
    def _():
        out_ref[...] = jnp.zeros_like(out_ref)


def place_update(owner_table, returned, mats):
    groups, rows, width = returned.shape

    def kernel(*refs):
        place_kernel(groups, *refs)

    return pl.pallas_call(
        kernel,
        grid_spec=pltpu.PrefetchScalarGridSpec(
            num_scalar_prefetch=1,
            grid=(mats,),
            in_specs=[
                pl.BlockSpec(
                    (1, rows, width), lambda k, owner: (jnp.minimum(owner[k], groups - 1), 0, 0)
                )
            ],
            out_specs=pl.BlockSpec((1, 1, rows, width), lambda k, owner: (k, 0, 0, 0)),
        ),
        out_shape=jax.ShapeDtypeStruct((mats, 1, rows, width), jnp.float32),
        cost_estimate=pl.CostEstimate(
            flops=0, bytes_accessed=4 * (groups + mats) * rows * width, transcendentals=0
        ),
    )(owner_table, returned)


def upper_gram(current):
    width = current.shape[1]
    size = width // STRIPES
    return jnp.concatenate(
        [
            dot3(
                current[:, i * size : (i + 1) * size],
                current[:, i * size :],
                (((0,), (0,)), ((), ())),
            )
            for i in range(STRIPES)
        ],
        axis=1,
    )


def triangle(packed):
    half = packed.shape[0] // 2
    parts, at = [], 0
    for i in range(STRIPES):
        end = at + (STRIPES - i) * 2 * half
        parts += [packed[:half, at:end], packed[half:, at + half : end]]
        at = end
    return jnp.concatenate(parts, axis=1)


def split(values):
    head = values.astype(jnp.bfloat16)
    return head, (values - head.astype(jnp.float32)).astype(jnp.bfloat16)


def product(left, right_head, right_tail):
    head, tail = split(left)
    whole = right_head[...]
    small = jnp.dot(head, right_tail[...], preferred_element_type=jnp.float32)
    small += jnp.dot(tail, whole, preferred_element_type=jnp.float32)
    return small + jnp.dot(head, whole, preferred_element_type=jnp.float32)


def polynomial_kernel(
    scale, packed_ref, head_ref, tail_ref, factor_ref, gram, gram_head, gram_tail, low, low_head, low_tail
):
    size = packed_ref.shape[0]
    width = gram.shape[0]
    count = width // size
    tile = min(256, width)

    total = jnp.zeros((size, size), jnp.float32)
    diagonal = lax.broadcasted_iota(jnp.int32, (size, size), 0) == lax.broadcasted_iota(
        jnp.int32, (size, size), 1
    )
    at = 0
    for i in range(count):
        total += jnp.where(diagonal, packed_ref[:, at : at + size], 0.0)
        at += (count - i) * size
    total = jnp.full((1, width), jnp.sum(total), jnp.float32)
    inverse = 1.0 / (jnp.sqrt(total) + norm_epsilon)
    square = inverse * inverse
    factor = inverse * scale
    factor_ref[...] = jnp.broadcast_to(first_coef * first_coef * factor, factor_ref.shape)

    at = 0
    for i in range(count):
        for j in range(i, count):
            block = packed_ref[:, at : at + size] * square[:, :size]
            at += size
            gram[i * size : (i + 1) * size, j * size : (j + 1) * size] = block
            if j > i:
                gram[j * size : (j + 1) * size, i * size : (i + 1) * size] = block.T

    @pl.loop(0, width // tile)
    def _(t):
        rows = pl.ds(pl.multiple_of(t * tile, tile), tile)
        gram_head[rows, :], gram_tail[rows, :] = split(gram[rows, :])

    @pl.loop(0, width // tile)
    def _(t):
        rows = pl.ds(pl.multiple_of(t * tile, tile), tile)
        own = gram[rows, :]
        values = second_coef * own + third_coef * product(own, gram_head, gram_tail)
        low[rows, :] = values
        low_head[rows, :], low_tail[rows, :] = split(values)

    @pl.loop(0, width // tile)
    def _(t):
        rows = pl.ds(pl.multiple_of(t * tile, tile), tile)
        own = gram[rows, :]
        own = first_coef * own + product(own, low_head, low_tail)
        own = first_coef * own + product(own, low_head, low_tail)
        gram[rows, :] = own
        gram_head[rows, :], gram_tail[rows, :] = split(own)

    @pl.loop(0, width // tile)
    def _(t):
        rows = pl.ds(pl.multiple_of(t * tile, tile), tile)
        own = gram[rows, :]
        high = second_coef * own + third_coef * product(own, gram_head, gram_tail)
        rest = first_coef * (low[rows, :] + high) + product(high, low_head, low_tail)
        head_ref[rows, :], tail_ref[rows, :] = split(rest * factor)


def polynomial(packed, width, scale):
    square = (width, width)

    def kernel(*refs):
        polynomial_kernel(scale, *refs)

    whole = pl.BlockSpec(memory_space=pltpu.VMEM)
    return pl.pallas_call(
        kernel,
        in_specs=[whole],
        out_specs=[whole] * 3,
        out_shape=[
            jax.ShapeDtypeStruct(square, jnp.bfloat16),
            jax.ShapeDtypeStruct(square, jnp.bfloat16),
            jax.ShapeDtypeStruct((8, width), jnp.float32),
        ],
        scratch_shapes=[
            pltpu.VMEM(square, jnp.float32),
            pltpu.VMEM(square, jnp.bfloat16),
            pltpu.VMEM(square, jnp.bfloat16),
        ]
        * 2,
        compiler_params=pltpu.CompilerParams(vmem_limit_bytes=40 * 2**20),
        cost_estimate=pl.CostEstimate(
            flops=30 * width**3, bytes_accessed=8 * width**2, transcendentals=0
        ),
    )(packed)


def apply_kernel(current_ref, head_ref, tail_ref, factor_ref, out_ref):
    values = current_ref[...]
    out_ref[...] = factor_ref[0:1, :] * values + product(values, head_ref, tail_ref)


def apply_polynomial(current, head, tail, factor):
    rows, width = current.shape
    tile = math.gcd(rows, 256)
    block = pl.BlockSpec((tile, width), lambda t: (t, 0))
    square = pl.BlockSpec((width, width), lambda t: (0, 0))
    return pl.pallas_call(
        apply_kernel,
        grid=(rows // tile,),
        in_specs=[block, square, square, pl.BlockSpec((8, width), lambda t: (0, 0))],
        out_specs=block,
        out_shape=jax.ShapeDtypeStruct((rows, width), jnp.float32),
        compiler_params=pltpu.CompilerParams(vmem_limit_bytes=32 * 2**20),
        cost_estimate=pl.CostEstimate(
            flops=6 * rows * width**2, bytes_accessed=8 * rows * width, transcendentals=0
        ),
    )(current, head, tail, factor)


def shards(grads, momentum, owner_table):
    mats = grads.shape[0]
    groups = lax.axis_size("far") * lax.axis_size("near")
    blocks = lax.axis_size("row")
    near = ("near", "row")
    in_window = owner_table < groups
    flags = in_window[:, None, None, None]
    group_ids = jnp.arange(groups, dtype=jnp.int32)
    matches = (owner_table[None, :] == group_ids[:, None]).astype(jnp.int32)
    chosen = jnp.sum(matches * jnp.arange(mats, dtype=jnp.int32)[None, :], axis=1)
    outgoing = pick_nesterov(chosen, grads, momentum, groups)
    rows, width = outgoing.shape[1:]
    owned = lax.all_to_all(outgoing, near, split_axis=0, concat_axis=0, tiled=True)
    new_momentum = jnp.where(flags, momentum_decay * momentum + grads, momentum)
    current = owned.reshape(groups * rows, width)
    scale = 0.2 * math.sqrt(max(rows * groups * blocks, width))
    packed = lax.psum(triangle(upper_gram(current)), "far")
    head, tail, factor = polynomial(packed, width, scale)
    result = apply_polynomial(current, head, tail, factor)
    returned = lax.all_to_all(
        result.reshape(groups, rows, width), near, split_axis=0, concat_axis=0, tiled=True
    )
    update = place_update(owner_table, returned, mats)
    return (new_momentum, update)


def solution(mesh):
    groups, blocks = mesh.shape["grp"], mesh.shape["row"]
    near = max(1, groups // blocks)
    assert near * blocks == groups
    split = Mesh(mesh.devices.reshape(groups // near, near, blocks), ("far", "near", "row"))
    spec = P(None, "row", ("far", "near"), None)
    return jax.shard_map(
        shards, mesh=split, in_specs=(spec, spec, P()), out_specs=(spec, spec), check_vma=False
    )
```

```python
import math

import jax
import jax.numpy as jnp
from jax import lax
from jax.experimental import pallas as pl
from jax.experimental.pallas import tpu as pltpu
from jax.sharding import Mesh
from jax.sharding import PartitionSpec as P

momentum_decay = 0.95
norm_epsilon = 1e-07
first_coef = 3.4445
second_coef = -4.775
third_coef = 2.0315

STRIPES = 4


def dot3(left, right, dims=(((1,), (0,)), ((), ()))):
    return lax.dot_general(
        left, right, dims, precision=lax.Precision.HIGH, preferred_element_type=jnp.float32
    )


def pick_kernel(chosen_ref, grads_ref, momentum_ref, out_ref):
    grad = grads_ref[0, 0]
    out_ref[0] = grad + momentum_decay * (momentum_decay * momentum_ref[0, 0] + grad)


def pick_nesterov(chosen, grads, momentum, groups):
    rows, width = grads.shape[2:]
    state = pl.BlockSpec((1, 1, rows, width), lambda g, chosen: (chosen[g], 0, 0, 0))
    return pl.pallas_call(
        pick_kernel,
        grid_spec=pltpu.PrefetchScalarGridSpec(
            num_scalar_prefetch=1,
            grid=(groups,),
            in_specs=[state, state],
            out_specs=pl.BlockSpec((1, rows, width), lambda g, chosen: (g, 0, 0)),
        ),
        out_shape=jax.ShapeDtypeStruct((groups, rows, width), jnp.float32),
        cost_estimate=pl.CostEstimate(
            flops=4 * groups * rows * width, bytes_accessed=12 * groups * rows * width, transcendentals=0
        ),
    )(chosen, grads, momentum)


def place_kernel(owner_ref, returned_ref, out_ref, zeros, sems):
    groups, mats = returned_ref.shape[0], out_ref.shape[0]
    zeros[...] = jnp.zeros_like(zeros)
    for k in range(mats):
        owner = owner_ref[k]
        slot = jnp.minimum(owner, groups - 1)

        @pl.when(owner < groups)
        def _(k=k, slot=slot):
            pltpu.make_async_copy(returned_ref.at[slot], out_ref.at[k, 0], sems.at[k]).start()

        @pl.when(owner >= groups)
        def _(k=k):
            pltpu.make_async_copy(zeros, out_ref.at[k, 0], sems.at[k]).start()

    for k in range(mats):
        pltpu.make_async_copy(zeros, out_ref.at[k, 0], sems.at[k]).wait()


def place_update(owner_table, returned, mats):
    groups, rows, width = returned.shape
    return pl.pallas_call(
        place_kernel,
        in_specs=[
            pl.BlockSpec(memory_space=pltpu.SMEM),
            pl.BlockSpec(memory_space=pltpu.VMEM),
        ],
        out_specs=pl.BlockSpec(memory_space=pl.ANY),
        out_shape=jax.ShapeDtypeStruct((mats, 1, rows, width), jnp.float32),
        scratch_shapes=[
            pltpu.VMEM((rows, width), jnp.float32),
            pltpu.SemaphoreType.DMA((mats,)),
        ],
        compiler_params=pltpu.CompilerParams(vmem_limit_bytes=32 * 2**20),
        cost_estimate=pl.CostEstimate(
            flops=0, bytes_accessed=4 * (groups + mats) * rows * width, transcendentals=0
        ),
    )(owner_table, returned)


def upper_gram(current):
    width = current.shape[1]
    size = width // STRIPES
    return jnp.concatenate(
        [
            dot3(
                current[:, i * size : (i + 1) * size],
                current[:, i * size :],
                (((0,), (0,)), ((), ())),
            )
            for i in range(STRIPES)
        ],
        axis=1,
    )


def triangle(packed):
    half = packed.shape[0] // 2
    parts, at = [], 0
    for i in range(STRIPES):
        end = at + (STRIPES - i) * 2 * half
        parts += [packed[:half, at:end], packed[half:, at + half : end]]
        at = end
    return jnp.concatenate(parts, axis=1)


def split(values):
    head = values.astype(jnp.bfloat16)
    return head, (values - head.astype(jnp.float32)).astype(jnp.bfloat16)


def product(left, right_head, right_tail):
    head, tail = split(left)
    whole = right_head[...]
    small = jnp.dot(head, right_tail[...], preferred_element_type=jnp.float32)
    small += jnp.dot(tail, whole, preferred_element_type=jnp.float32)
    return small + jnp.dot(head, whole, preferred_element_type=jnp.float32)


def polynomial_kernel(
    scale, packed_ref, head_ref, tail_ref, factor_ref, gram, gram_head, gram_tail, low, low_head, low_tail
):
    size = packed_ref.shape[0]
    width = gram.shape[0]
    count = width // size
    tile = min(256, width)

    total = jnp.zeros((size, size), jnp.float32)
    diagonal = lax.broadcasted_iota(jnp.int32, (size, size), 0) == lax.broadcasted_iota(
        jnp.int32, (size, size), 1
    )
    at = 0
    for i in range(count):
        total += jnp.where(diagonal, packed_ref[:, at : at + size], 0.0)
        at += (count - i) * size
    total = jnp.full((1, width), jnp.sum(total), jnp.float32)
    inverse = 1.0 / (jnp.sqrt(total) + norm_epsilon)
    square = inverse * inverse
    factor = inverse * scale
    factor_ref[...] = jnp.broadcast_to(first_coef * first_coef * factor, factor_ref.shape)

    at = 0
    for i in range(count):
        for j in range(i, count):
            block = packed_ref[:, at : at + size] * square[:, :size]
            at += size
            gram[i * size : (i + 1) * size, j * size : (j + 1) * size] = block
            if j > i:
                gram[j * size : (j + 1) * size, i * size : (i + 1) * size] = block.T

    @pl.loop(0, width // tile)
    def _(t):
        rows = pl.ds(pl.multiple_of(t * tile, tile), tile)
        gram_head[rows, :], gram_tail[rows, :] = split(gram[rows, :])

    @pl.loop(0, width // tile)
    def _(t):
        rows = pl.ds(pl.multiple_of(t * tile, tile), tile)
        own = gram[rows, :]
        values = second_coef * own + third_coef * product(own, gram_head, gram_tail)
        low[rows, :] = values
        low_head[rows, :], low_tail[rows, :] = split(values)

    @pl.loop(0, width // tile)
    def _(t):
        rows = pl.ds(pl.multiple_of(t * tile, tile), tile)
        own = gram[rows, :]
        own = first_coef * own + product(own, low_head, low_tail)
        own = first_coef * own + product(own, low_head, low_tail)
        gram[rows, :] = own
        gram_head[rows, :], gram_tail[rows, :] = split(own)

    @pl.loop(0, width // tile)
    def _(t):
        rows = pl.ds(pl.multiple_of(t * tile, tile), tile)
        own = gram[rows, :]
        high = second_coef * own + third_coef * product(own, gram_head, gram_tail)
        rest = first_coef * (low[rows, :] + high) + product(high, low_head, low_tail)
        head_ref[rows, :], tail_ref[rows, :] = split(rest * factor)


def polynomial(packed, width, scale):
    square = (width, width)

    def kernel(*refs):
        polynomial_kernel(scale, *refs)

    whole = pl.BlockSpec(memory_space=pltpu.VMEM)
    return pl.pallas_call(
        kernel,
        in_specs=[whole],
        out_specs=[whole] * 3,
        out_shape=[
            jax.ShapeDtypeStruct(square, jnp.bfloat16),
            jax.ShapeDtypeStruct(square, jnp.bfloat16),
            jax.ShapeDtypeStruct((8, width), jnp.float32),
        ],
        scratch_shapes=[
            pltpu.VMEM(square, jnp.float32),
            pltpu.VMEM(square, jnp.bfloat16),
            pltpu.VMEM(square, jnp.bfloat16),
        ]
        * 2,
        compiler_params=pltpu.CompilerParams(vmem_limit_bytes=40 * 2**20),
        cost_estimate=pl.CostEstimate(
            flops=30 * width**3, bytes_accessed=8 * width**2, transcendentals=0
        ),
    )(packed)


def apply_kernel(current_ref, head_ref, tail_ref, factor_ref, out_ref):
    values = current_ref[...]
    out_ref[...] = factor_ref[0:1, :] * values + product(values, head_ref, tail_ref)


def apply_polynomial(current, head, tail, factor):
    rows, width = current.shape
    tile = math.gcd(rows, 256)
    block = pl.BlockSpec((tile, width), lambda t: (t, 0))
    square = pl.BlockSpec((width, width), lambda t: (0, 0))
    return pl.pallas_call(
        apply_kernel,
        grid=(rows // tile,),
        in_specs=[block, square, square, pl.BlockSpec((8, width), lambda t: (0, 0))],
        out_specs=block,
        out_shape=jax.ShapeDtypeStruct((rows, width), jnp.float32),
        compiler_params=pltpu.CompilerParams(vmem_limit_bytes=32 * 2**20),
        cost_estimate=pl.CostEstimate(
            flops=6 * rows * width**2, bytes_accessed=8 * rows * width, transcendentals=0
        ),
    )(current, head, tail, factor)


def shards(grads, momentum, owner_table):
    mats = grads.shape[0]
    groups = lax.axis_size("far") * lax.axis_size("near")
    blocks = lax.axis_size("row")
    near = ("near", "row")
    in_window = owner_table < groups
    flags = in_window[:, None, None, None]
    group_ids = jnp.arange(groups, dtype=jnp.int32)
    matches = (owner_table[None, :] == group_ids[:, None]).astype(jnp.int32)
    chosen = jnp.sum(matches * jnp.arange(mats, dtype=jnp.int32)[None, :], axis=1)
    outgoing = pick_nesterov(chosen, grads, momentum, groups)
    rows, width = outgoing.shape[1:]
    owned = lax.all_to_all(outgoing, near, split_axis=0, concat_axis=0, tiled=True)
    new_momentum = jnp.where(flags, momentum_decay * momentum + grads, momentum)
    current = owned.reshape(groups * rows, width)
    scale = 0.2 * math.sqrt(max(rows * groups * blocks, width))
    packed = lax.psum(triangle(upper_gram(current)), "far")
    head, tail, factor = polynomial(packed, width, scale)
    result = apply_polynomial(current, head, tail, factor)
    returned = lax.all_to_all(
        result.reshape(groups, rows, width), near, split_axis=0, concat_axis=0, tiled=True
    )
    update = place_update(owner_table, returned, mats)
    return (new_momentum, update)


def solution(mesh):
    groups, blocks = mesh.shape["grp"], mesh.shape["row"]
    near = max(1, groups // blocks)
    assert near * blocks == groups
    split = Mesh(mesh.devices.reshape(groups // near, near, blocks), ("far", "near", "row"))
    spec = P(None, "row", ("far", "near"), None)
    return jax.shard_map(
        shards, mesh=split, in_specs=(spec, spec, P()), out_specs=(spec, spec), check_vma=False
    )
```
